32 devices in a mesh: img: 4 (over y, core), tile: 8 (over z, x).
Axes of the slice: x: 2, y: 2, z: 4, core: 2. Of those that a mesh axis runs over, the one named last changes fastest.
Arguments:
- tiles: bfloat16 [8192, 1152], P(('img', 'tile')), may hold values from -6 to 6
- tile_image: int32 [32], P(('img', 'tile')), may hold values from 0 to 1
- guide: bfloat16 [8, 512, 1152], P('img', 'tile'), may hold values from -160 to 160
- gain: float32 [1152], replicated, may hold values from 0.5 to 1.5
- w_query: bfloat16 [1152, 1152], replicated, may hold values from -0.1875 to 0.1875
- w_key: bfloat16 [1152, 1152], replicated, may hold values from -0.1875 to 0.1875
- w_value: bfloat16 [1152, 1152], replicated, may hold values from -0.1875 to 0.1875
- w_out: bfloat16 [1152, 1152], replicated, may hold values from -0.1875 to 0.1875
- grad_out: bfloat16 [8192, 1152], P(('img', 'tile')), may hold values from -6 to 6
Outputs:
- grad_tiles: bfloat16 [8192, 1152], P(('img', 'tile'))
- grad_guide: bfloat16 [8, 512, 1152], P('img', 'tile')
- grad_weights: float32 [4, 1152, 1152], P(None, ('img', 'tile'))
- grad_gain: float32 [1152], replicated
The draws below stay inside these ranges and needn't reach their ends.
Inputs may be any that keep to these rules, and one draw needn't show every extreme that they name: `tile_image`: image of each tile within its own img group of 2 images.
All inputs are finite; a program needn't handle non-finite values.
Results may differ from the reference program's by a relative error of at most 0.034.
The reference program's roundings to bfloat16 on the way count: a program that leaves them out, or rounds other values in their place, can miss the bound.
Values may be sent and summed in bfloat16 or wider, within the bound.
A program may use at most 128 MiB of HBM per device.

```python
import jax
import jax.numpy as jnp
from jax import lax

D = 1152
HEADS = 16
TILE = 256
IMG_GRP = 2
G = 512
TILES = 32
TOKENS = 8192
IMAGES = 8
N_IMG = 4


def draw_guide(key, part):
    base_key = jax.random.fold_in(key, 11)
    values = jax.random.normal(base_key, (IMAGES, G, D), jnp.float32)
    return jnp.clip(values, -160.0, 160.0).astype(jnp.bfloat16)


def touch_ends(result, stream_key, smallest, top_value):
    spot = [jax.random.randint(jax.random.fold_in(stream_key, axis), (), 0, length) for axis, length in enumerate(result.shape)]
    widest = result.shape.index(max(result.shape))
    next_to = spot[:widest] + [(spot[widest] + 1) % result.shape[widest]] + spot[widest + 1:]
    return result.at[tuple(spot)].set(smallest).at[tuple(next_to)].set(top_value)


def strengthened(result, rng, source, target, shards_of, factor):
    owner, partner = [(jnp.arange(result.shape[axis_at]) // (result.shape[axis_at] // shards_of)).reshape([-1 if axis == axis_at else 1 for axis in range(result.ndim)]) for axis_at in (source, target)]
    chosen = jax.random.permutation(rng, shards_of)[partner]
    strong = (owner == chosen) | (owner == (partner + shards_of // 2) % shards_of)
    return jnp.where(strong, factor * result, result)


def levels(key, shape, shards, least, top_value):
    level, own = 1.0, jax.random.fold_in(key, 6)
    for axis_at, blocks in shards:
        draws = jnp.exp(jax.random.uniform(jax.random.fold_in(own, axis_at), (blocks,), jnp.float32, least / len(shards), top_value / len(shards)))
        level = level * jnp.repeat(draws, shape[axis_at] // blocks).reshape([-1 if axis == axis_at else 1 for axis in range(len(shape))])
    return level


def gaussian(rng, extent, deviation, limit, pieces=(), held_as=jnp.bfloat16):
    level = levels(rng, extent, pieces, -0.22, 0.18) if pieces else 1.0
    values = jax.random.normal(rng, extent, jnp.float32) * deviation * level
    return jnp.minimum(jnp.maximum(values, -limit), limit).astype(held_as)


def gaussian_with(stream_key, dims, deviation, reach, cuts, heavy, kind=jnp.bfloat16):
    result = deviation * jax.random.normal(stream_key, dims, jnp.float32)
    if cuts:
        result = result * levels(stream_key, dims, cuts, -0.22, 0.18)
    return jnp.clip(strengthened(result, jax.random.fold_in(stream_key, 3), *heavy), -reach, reach).astype(kind)


def setup_inputs(seed: int = 0) -> dict:
    key_list = jax.random.split(jax.random.key(seed), 10)
    return {
        "tiles": gaussian(key_list[0], (TOKENS, D), 1.0, 6.0, ((0, 32),)),
        "tile_image": touch_ends(jax.random.randint(key_list[1], (TILES,), 0, IMG_GRP), jax.random.fold_in(key_list[1], 1), 0, IMG_GRP - 1).astype(jnp.int32),
        "guide": draw_guide(jax.random.fold_in(key_list[9], 71), 0),
        "gain": jnp.clip(1.0 + 0.1 * jax.random.normal(key_list[3], (D,), jnp.float32), 0.5, 1.5),
        "w_query": gaussian(key_list[4], (D, D), D ** -0.5, 0.1875),
        "w_key": gaussian(key_list[5], (D, D), D ** -0.5, 0.1875),
        "w_value": gaussian(key_list[6], (D, D), D ** -0.5, 0.1875),
        "w_out": gaussian(key_list[7], (D, D), D ** -0.5, 0.1875),
        "grad_out": gaussian_with(key_list[8], (TOKENS, D), 1.0, 6.0, ((0, 32),), (0, 1, 32, 2.75)),
    }


def tile_pass(q_tile, k_img, v_img, d_tile):
    head_size = D // HEADS
    scale = head_size ** (-0.5)
    qh = q_tile.reshape(TILE, HEADS, head_size).astype(jnp.float32)
    kh = k_img.reshape(G, HEADS, head_size).astype(jnp.float32)
    vh = v_img.reshape(G, HEADS, head_size).astype(jnp.float32)
    dh = d_tile.reshape(TILE, HEADS, head_size).astype(jnp.float32)
    scores = jnp.einsum('qhd,khd->hqk', qh, kh) * scale
    top = lax.optimization_barrier(jnp.max(scores, axis=-1, keepdims=True))
    expo = jnp.exp(scores - top)
    probs = expo / lax.optimization_barrier(jnp.sum(expo, axis=-1, keepdims=True))
    pb = probs.astype(jnp.bfloat16)
    outv = jnp.einsum('hqk,khd->qhd', pb.astype(jnp.float32), vh).astype(jnp.bfloat16)
    dprob = jnp.einsum('qhd,khd->hqk', dh, vh)
    delta = lax.optimization_barrier(jnp.sum(probs * dprob, axis=-1, keepdims=True))
    dscore = (probs * (dprob - delta) * scale).astype(jnp.bfloat16).astype(jnp.float32)
    dq = jnp.einsum('hqk,khd->qhd', dscore, kh).astype(jnp.bfloat16)
    dk = jnp.einsum('hqk,qhd->khd', dscore, qh).reshape(G, D)
    dv = jnp.einsum('hqk,qhd->khd', pb.astype(jnp.float32), dh).reshape(G, D)
    return (outv.reshape(TILE, D), dq.reshape(TILE, D), dk, dv)

def reference(tiles, tile_image, guide, gain, w_query, w_key, w_value, w_out, grad_out):
    xf = tiles.astype(jnp.float32)
    rstd = lax.rsqrt(lax.optimization_barrier(jnp.mean(xf * xf, axis=-1, keepdims=True)) + 1e-06)
    normed = xf * rstd
    hidden = (normed * gain).astype(jnp.bfloat16)
    query = jnp.dot(hidden, w_query, preferred_element_type=jnp.float32).astype(jnp.bfloat16)
    flat = guide.reshape(IMAGES * G, D)
    keys = jnp.dot(flat, w_key, preferred_element_type=jnp.float32).astype(jnp.bfloat16).reshape(IMAGES, G, D)
    values = jnp.dot(flat, w_value, preferred_element_type=jnp.float32).astype(jnp.bfloat16).reshape(IMAGES, G, D)
    dout = jnp.dot(grad_out, w_out.T, preferred_element_type=jnp.float32).astype(jnp.bfloat16)
    group = (jnp.arange(TILES, dtype=jnp.int32) // (TILES // N_IMG)).astype(jnp.int32)
    owner = (group * IMG_GRP + tile_image).astype(jnp.int32)

    def step(carry, item):
        dk_acc, dv_acc = carry
        q_tile, d_tile, image = item
        k_img = lax.dynamic_index_in_dim(keys, image, 0, keepdims=False)
        v_img = lax.dynamic_index_in_dim(values, image, 0, keepdims=False)
        outv, dq, dk, dv = tile_pass(q_tile, k_img, v_img, d_tile)
        old_k = lax.dynamic_index_in_dim(dk_acc, image, 0, keepdims=False)
        old_v = lax.dynamic_index_in_dim(dv_acc, image, 0, keepdims=False)
        dk_acc = lax.dynamic_update_index_in_dim(dk_acc, old_k + dk, image, 0)
        dv_acc = lax.dynamic_update_index_in_dim(dv_acc, old_v + dv, image, 0)
        return ((dk_acc, dv_acc), (outv, dq))
    start = (jnp.zeros((IMAGES, G, D), jnp.float32), jnp.zeros((IMAGES, G, D), jnp.float32))
    (dk_all, dv_all), (outs, dqs) = lax.scan(step, start, (query.reshape(TILES, TILE, D), dout.reshape(TILES, TILE, D), owner))
    outv = outs.reshape(TOKENS, D)
    dq = dqs.reshape(TOKENS, D)
    dkb = dk_all.astype(jnp.bfloat16).reshape(IMAGES * G, D)
    dvb = dv_all.astype(jnp.bfloat16).reshape(IMAGES * G, D)
    grad_guide = (jnp.dot(dkb, w_key.T, preferred_element_type=jnp.float32) + jnp.dot(dvb, w_value.T, preferred_element_type=jnp.float32)).astype(jnp.bfloat16).reshape(IMAGES, G, D)
    grad_weights = jnp.stack([jnp.dot(hidden.T, dq, preferred_element_type=jnp.float32), jnp.dot(flat.T, dkb, preferred_element_type=jnp.float32), jnp.dot(flat.T, dvb, preferred_element_type=jnp.float32), jnp.dot(outv.T, grad_out, preferred_element_type=jnp.float32)])
    dh = jnp.dot(dq, w_query.T, preferred_element_type=jnp.float32)
    grad_gain = lax.optimization_barrier(jnp.sum(dh * normed, axis=0))
    dn = dh * gain
    grad_tiles = (rstd * (dn - normed * lax.optimization_barrier(jnp.mean(dn * normed, axis=-1, keepdims=True)))).astype(jnp.bfloat16)
    return (grad_tiles, grad_guide, grad_weights, grad_gain)
```

```python
import functools

import jax
import jax.numpy as jnp
import numpy as np
from jax import lax
from jax.experimental import pallas as pl
from jax.experimental.pallas import tpu as pltpu
from jax.sharding import PartitionSpec as P

HEADS = 16
TILE = 256
LANES = 128
AXES = ("img", "tile")
BF = jnp.bfloat16
F32 = jnp.float32


def nt(a, b):
    return lax.dot_general(a, b, (((1,), (1,)), ((), ())), preferred_element_type=F32)


def tn(a, b):
    return lax.dot_general(a, b, (((0,), (0,)), ((), ())), preferred_element_type=F32)


def nn(a, b):
    return jnp.dot(a, b, preferred_element_type=F32)


def attention_kernel(q_ref, d_ref, k_ref, v_ref, o_ref, dq_ref, dk_ref, dv_ref):
    width = q_ref.shape[1]
    size = width // HEADS
    scale = size ** (-0.5)

    def put(ref, first, cols, inside, value):
        value = value.astype(ref.dtype)
        if first:
            value = jnp.where(inside, value, ref[:, cols])
        ref[:, cols] = value

    for head in range(HEADS):
        low = head * size // LANES * LANES
        high = -(-(head + 1) * size // LANES) * LANES
        first = head * size - low
        cols = slice(low, high)
        lane = lax.broadcasted_iota(jnp.int32, (1, high - low), 1)
        inside = lane >= first
        mine = inside & (lane < first + size)
        q = jnp.where(mine, q_ref[:, cols], jnp.zeros((), BF))
        d = jnp.where(mine, d_ref[:, cols], jnp.zeros((), BF))
        k = k_ref[:, cols]
        v = v_ref[:, cols]
        scores = nt(q, k) * scale
        top = jnp.max(scores, axis=-1, keepdims=True)
        expo = jnp.exp(scores - top)
        probs = expo * (1.0 / jnp.sum(expo, axis=-1, keepdims=True))
        pb = probs.astype(BF)
        put(o_ref, first, cols, inside, nn(pb, v))
        dprob = nt(d, v)
        delta = jnp.sum(probs * dprob, axis=-1, keepdims=True)
        ds = (probs * (dprob - delta) * scale).astype(BF)
        put(dq_ref, first, cols, inside, nn(ds, k))
        put(dk_ref, first, cols, inside, tn(ds, q))
        put(dv_ref, first, cols, inside, tn(pb, d))


def attention(q, d, k, v):
    rows, width = q.shape
    keyrows = k.shape[0]
    vmem = pl.BlockSpec(memory_space=pltpu.VMEM)
    flops = 12 * rows * keyrows * width
    return pl.pallas_call(
        attention_kernel,
        out_shape=(
            jax.ShapeDtypeStruct((rows, width), BF),
            jax.ShapeDtypeStruct((rows, width), BF),
            jax.ShapeDtypeStruct((keyrows, width), BF),
            jax.ShapeDtypeStruct((keyrows, width), BF),
        ),
        in_specs=[vmem] * 4,
        out_specs=(vmem,) * 4,
        compiler_params=pltpu.CompilerParams(vmem_limit_bytes=40 * 2**20),
        cost_estimate=pl.CostEstimate(
            flops=4 * flops,
            bytes_accessed=2 * (4 * rows + 4 * keyrows) * width,
            transcendentals=HEADS * rows * keyrows,
        ),
        name="attention",
    )(q, d, k, v)


def on_device(n_img, n_tile, tiles, tile_image, guide, gain, w_query, w_key, w_value, w_out, grad_out):
    width = tiles.shape[1]
    images, part = guide.shape[0], guide.shape[1]
    i = lax.axis_index("img")
    t = lax.axis_index("tile")
    image = tile_image[0]
    tile_bits = [1 << b for b in range(n_tile.bit_length() - 1)]
    img_bits = [1 << b for b in range(n_img.bit_length() - 1)]

    def swap_tile(x, bit):
        return lax.ppermute(x, "tile", [(s, s ^ bit) for s in range(n_tile)])

    def swap_img(x, bit):
        return lax.ppermute(x, "img", [(s, s ^ bit) for s in range(n_img)])

    theirs = swap_tile(tile_image, 1)[0]
    blocks = guide[None]
    for bit in tile_bits[:0:-1]:
        blocks = jnp.concatenate([blocks, swap_tile(blocks, bit)], axis=0)

    def pick(arr, which):
        chosen = arr[:, 0]
        for c in range(1, images):
            chosen = jnp.where(which == c, arr[:, c], chosen)
        return chosen

    other = swap_tile(pick(blocks, theirs), 1)
    mine = pick(blocks, image)
    used = jnp.concatenate([mine, other], axis=0).reshape(-1, width)

    xf = tiles.astype(F32)
    rstd = lax.rsqrt(jnp.mean(xf * xf, axis=-1, keepdims=True) + 1e-06)
    normed = xf * rstd
    hidden = (normed * gain).astype(BF)
    query = nn(hidden, w_query).astype(BF)
    dout = nt(grad_out, w_out).astype(BF)
    keys = nn(used, w_key).astype(BF)
    values = nn(used, w_value).astype(BF)
    outv, dq, dk, dv = attention(query, dout, keys, values)

    r = width // (n_img * n_tile)
    order = np.arange(width).reshape(n_img, n_tile // 2, 2, r).transpose(2, 0, 1, 3).reshape(-1)
    onehot = (
        lax.broadcasted_iota(jnp.int32, (width, width), 0) == jnp.asarray(order, jnp.int32)[None]
    ).astype(BF)

    def reduced(left, right, tile_first):
        ordered = nn(left, onehot).astype(BF)
        x = tn(ordered, right).astype(BF)
        x = x.reshape(2, n_img // 2, 2, width // (2 * n_img), width)

        def halve(x, axis, bit, swap):
            keep = lax.dynamic_index_in_dim(x, bit, axis, keepdims=False)
            send = lax.dynamic_index_in_dim(x, 1 - bit, axis, keepdims=False)
            return (keep.astype(F32) + swap(send).astype(F32)).astype(BF)

        x = halve(x, 2, i & 1, lambda s: swap_img(s, 1))
        steps = [("img", bit) for bit in img_bits[1:]]
        steps = [("tile", 1)] + steps if tile_first else steps + [("tile", 1)]
        lead_tile = True
        for name, bit in steps:
            if name == "tile":
                x = halve(x, 0, t & 1, lambda s: swap_tile(s, 1))
                lead_tile = False
            else:
                axis = 1 if lead_tile else 0
                shape = x.shape
                x = x.reshape(shape[:axis] + (shape[axis] // 2, 2) + shape[axis + 1 :])
                x = halve(x, axis + 1, (i // bit) & 1, lambda s, bit=bit: swap_img(s, bit))
        x = x.reshape(n_tile // 2, r, width)
        for bit in tile_bits[1:]:
            x = x.reshape(x.shape[0] // 2, 2, r, width)
            x = halve(x, 1, (t // bit) & 1, lambda s, bit=bit: swap_tile(s, bit))
        return x.reshape(r, width).astype(F32)

    grad_out_w = reduced(outv, grad_out, False)
    grad_query_w = reduced(hidden, dq, True)

    term = (nt(dk, w_key) + nt(dv, w_value)).astype(BF).reshape(n_tile, part, width)
    half = n_tile // 2
    received = swap_tile(term[half:], 1).astype(F32)
    own = term[:half].astype(F32)
    x = jnp.stack(
        [jnp.where(image == c, own, 0.0) + jnp.where(theirs == c, received, 0.0) for c in range(images)],
        axis=1,
    ).astype(BF)
    for bit in tile_bits[1:]:
        half = x.shape[0] // 2
        x = (x[:half].astype(F32) + swap_tile(x[half:], bit).astype(F32)).astype(BF)
    grad_guide = x.reshape(guide.shape)

    grad_key_w = reduced(used, dk, False)
    grad_value_w = reduced(used, dv, True)

    dh = nt(dq, w_query)
    grad_gain = jnp.sum(dh * normed, axis=0)
    for bit in tile_bits:
        grad_gain = grad_gain + swap_tile(grad_gain, bit)
    for bit in img_bits:
        grad_gain = grad_gain + swap_img(grad_gain, bit)
    dn = dh * gain
    grad_tiles = (rstd * (dn - normed * jnp.mean(dn * normed, axis=-1, keepdims=True))).astype(BF)
    grad_weights = jnp.stack([grad_query_w, grad_key_w, grad_value_w, grad_out_w])
    return (grad_tiles, grad_guide, grad_weights, grad_gain)


def solution(mesh):
    return jax.shard_map(
        functools.partial(on_device, mesh.shape["img"], mesh.shape["tile"]),
        mesh=mesh,
        in_specs=(
            P(("img", "tile"), None),
            P(("img", "tile")),
            P("img", "tile", None),
            P(),
            P(),
            P(),
            P(),
            P(),
            P(("img", "tile"), None),
        ),
        out_specs=(
            P(("img", "tile"), None),
            P("img", "tile", None),
            P(None, ("img", "tile"), None),
            P(),
        ),
        check_vma=False,
    )
```

```python
import functools

import jax
import jax.numpy as jnp
import numpy as np
from jax import lax
from jax.experimental import pallas as pl
from jax.experimental.pallas import tpu as pltpu
from jax.sharding import PartitionSpec as P

HEADS = 16
TILE = 256
LANES = 128
AXES = ("img", "tile")
BF = jnp.bfloat16
F32 = jnp.float32


def nt(a, b):
    return lax.dot_general(a, b, (((1,), (1,)), ((), ())), preferred_element_type=F32)


def tn(a, b):
    return lax.dot_general(a, b, (((0,), (0,)), ((), ())), preferred_element_type=F32)


def nn(a, b):
    return jnp.dot(a, b, preferred_element_type=F32)


def attention_kernel(q_ref, d_ref, k_ref, v_ref, o_ref, dq_ref, dk_ref, dv_ref):
    width = q_ref.shape[1]
    size = width // HEADS
    scale = size ** (-0.5)

    def put(ref, first, cols, inside, value):
        value = value.astype(ref.dtype)
        if first:
            value = jnp.where(inside, value, ref[:, cols])
        ref[:, cols] = value

    for head in range(HEADS):
        low = head * size // LANES * LANES
        high = -(-(head + 1) * size // LANES) * LANES
        first = head * size - low
        cols = slice(low, high)
        lane = lax.broadcasted_iota(jnp.int32, (1, high - low), 1)
        inside = lane >= first
        mine = inside & (lane < first + size)
        q = jnp.where(mine, q_ref[:, cols], jnp.zeros((), BF))
        d = jnp.where(mine, d_ref[:, cols], jnp.zeros((), BF))
        k = k_ref[:, cols]
        v = v_ref[:, cols]
        scores = nt(q, k) * scale
        top = jnp.max(scores, axis=-1, keepdims=True)
        expo = jnp.exp(scores - top)
        probs = expo * (1.0 / jnp.sum(expo, axis=-1, keepdims=True))
        pb = probs.astype(BF)
        put(o_ref, first, cols, inside, nn(pb, v))
        dprob = nt(d, v)
        delta = jnp.sum(probs * dprob, axis=-1, keepdims=True)
        ds = (probs * (dprob - delta) * scale).astype(BF)
        put(dq_ref, first, cols, inside, nn(ds, k))
        put(dk_ref, first, cols, inside, tn(ds, q))
        put(dv_ref, first, cols, inside, tn(pb, d))


def attention(q, d, k, v):
    rows, width = q.shape
    keyrows = k.shape[0]
    vmem = pl.BlockSpec(memory_space=pltpu.VMEM)
    flops = 12 * rows * keyrows * width
    return pl.pallas_call(
        attention_kernel,
        out_shape=(
            jax.ShapeDtypeStruct((rows, width), BF),
            jax.ShapeDtypeStruct((rows, width), BF),
            jax.ShapeDtypeStruct((keyrows, width), BF),
            jax.ShapeDtypeStruct((keyrows, width), BF),
        ),
        in_specs=[vmem] * 4,
        out_specs=(vmem,) * 4,
        compiler_params=pltpu.CompilerParams(vmem_limit_bytes=40 * 2**20),
        cost_estimate=pl.CostEstimate(
            flops=4 * flops,
            bytes_accessed=2 * (4 * rows + 4 * keyrows) * width,
            transcendentals=HEADS * rows * keyrows,
        ),
        name="attention",
    )(q, d, k, v)


def on_device(n_img, n_tile, tiles, tile_image, guide, gain, w_query, w_key, w_value, w_out, grad_out):
    width = tiles.shape[1]
    images, part = guide.shape[0], guide.shape[1]
    i = lax.axis_index("img")
    t = lax.axis_index("tile")
    image = tile_image[0]
    tile_bits = [1 << b for b in range(n_tile.bit_length() - 1)]
    img_bits = [1 << b for b in range(n_img.bit_length() - 1)]

    def swap_tile(x, bit):
        return lax.ppermute(x, "tile", [(s, s ^ bit) for s in range(n_tile)])

    def swap_img(x, bit):
        return lax.ppermute(x, "img", [(s, s ^ bit) for s in range(n_img)])

    def pick(arr, which):
        chosen = arr[0]
        for c in range(1, images):
            chosen = jnp.where(which == c, arr[c], chosen)
        return chosen

    exchange = tile_bits[1:2] + tile_bits[:1] + tile_bits[2:]
    codes = [0]
    for bit in reversed(exchange):
        codes = codes + [c | bit for c in codes]
    theirs = swap_tile(tile_image, 1)[0]
    first_image = swap_tile(tile_image, exchange[0])[0]
    pieces = {}
    for code in sorted((c for c in range(0, n_tile, 2)), key=lambda c: (c != 0, -c)):
        block = swap_tile(guide, code) if code else guide
        pieces[code] = pick(block, image)
        pieces[code | 1] = swap_tile(pick(block, theirs), 1)
    used = jnp.concatenate([pieces[c] for c in codes], axis=0)

    xf = tiles.astype(F32)
    rstd = lax.rsqrt(jnp.mean(xf * xf, axis=-1, keepdims=True) + 1e-06)
    normed = xf * rstd
    hidden = (normed * gain).astype(BF)
    r = width // (n_img * n_tile)
    order = np.arange(width).reshape(n_img, n_tile // 2, 2, r).transpose(2, 0, 1, 3).reshape(-1)
    onehot = (
        lax.broadcasted_iota(jnp.int32, (width, width), 0) == jnp.asarray(order, jnp.int32)[None]
    ).astype(BF)

    query = nn(hidden, w_query).astype(BF)
    dout = nt(grad_out, w_out).astype(BF)
    hidden_ordered = nn(hidden, onehot).astype(BF)
    query, dout, hidden_ordered = lax.optimization_barrier((query, dout, hidden_ordered))
    keys = nn(used, w_key).astype(BF)
    values = nn(used, w_value).astype(BF)
    outv, dq, dk, dv = attention(query, dout, keys, values)

    def halve(x, axis, bit, swap):
        keep = lax.dynamic_index_in_dim(x, bit, axis, keepdims=False)
        send = lax.dynamic_index_in_dim(x, 1 - bit, axis, keepdims=False)
        return (keep.astype(F32) + swap(send).astype(F32)).astype(BF)

    def first_half(ordered, right):
        x = tn(ordered, right).astype(BF)
        x = x.reshape(2, n_img // 2, 2, width // (2 * n_img), width)
        return halve(x, 2, i & 1, lambda s: swap_img(s, 1))

    def reduced(x, tile_first):
        steps = [("img", bit) for bit in img_bits[1:]]
        steps = [("tile", 1)] + steps if tile_first else steps + [("tile", 1)]
        lead_tile = True
        for name, bit in steps:
            if name == "tile":
                x = halve(x, 0, t & 1, lambda s: swap_tile(s, 1))
                lead_tile = False
            else:
                axis = 1 if lead_tile else 0
                shape = x.shape
                x = x.reshape(shape[:axis] + (shape[axis] // 2, 2) + shape[axis + 1 :])
                x = halve(x, axis + 1, (i // bit) & 1, lambda s, bit=bit: swap_img(s, bit))
        x = x.reshape(n_tile // 2, r, width)
        total = lax.dynamic_index_in_dim(x, t // 2, 0, keepdims=False).astype(F32)
        for code in range(n_tile - 2, 0, -2):
            send = lax.dynamic_index_in_dim(x, (t ^ code) // 2, 0, keepdims=False)
            total = total + swap_tile(send, code).astype(F32)
        return total

    def after(x, *done):
        return lax.optimization_barrier((x,) + done)[0]

    half_out = first_half(nn(outv, onehot).astype(BF), grad_out)
    half_query = first_half(hidden_ordered, dq)
    used_ordered = nn(used, onehot).astype(BF)
    half_key = first_half(used_ordered, after(dk, half_out))
    half_value = first_half(used_ordered, after(dv, half_query))
    dk, dv = after(dk, half_key), after(dv, half_key)
    dq = after(dq, half_value)
    grad_out_w = reduced(half_out, False)
    grad_query_w = reduced(half_query, True)
    grad_key_w = reduced(half_key, False)
    grad_value_w = reduced(half_value, False)

    term = (nt(dk, w_key) + nt(dv, w_value)).astype(BF).reshape(n_tile, part, width)
    half = n_tile // 2
    received = swap_tile(term[half:], exchange[0]).astype(F32)
    own = term[:half].astype(F32)
    x = jnp.stack(
        [
            jnp.where(image == c, own, 0.0) + jnp.where(first_image == c, received, 0.0)
            for c in range(images)
        ],
        axis=1,
    ).astype(BF)
    for bit in exchange[1:]:
        half = x.shape[0] // 2
        x = (x[:half].astype(F32) + swap_tile(x[half:], bit).astype(F32)).astype(BF)
    grad_guide = x.reshape(guide.shape)

    dh = nt(dq, w_query)
    grad_gain = jnp.sum(dh * normed, axis=0)
    for bit in tile_bits:
        grad_gain = grad_gain + swap_tile(grad_gain, bit)
    for bit in img_bits:
        grad_gain = grad_gain + swap_img(grad_gain, bit)
    dn = dh * gain
    grad_tiles = (rstd * (dn - normed * jnp.mean(dn * normed, axis=-1, keepdims=True))).astype(BF)
    grad_weights = jnp.stack([grad_query_w, grad_key_w, grad_value_w, grad_out_w])
    return (grad_tiles, grad_guide, grad_weights, grad_gain)


def solution(mesh):
    return jax.shard_map(
        functools.partial(on_device, mesh.shape["img"], mesh.shape["tile"]),
        mesh=mesh,
        in_specs=(
            P(("img", "tile"), None),
            P(("img", "tile")),
            P("img", "tile", None),
            P(),
            P(),
            P(),
            P(),
            P(),
            P(("img", "tile"), None),
        ),
        out_specs=(
            P(("img", "tile"), None),
            P("img", "tile", None),
            P(None, ("img", "tile"), None),
            P(),
        ),
        check_vma=False,
    )
```

```python
import functools

import jax
import jax.numpy as jnp
import numpy as np
from jax import lax
from jax.experimental import pallas as pl
from jax.experimental.pallas import tpu as pltpu
from jax.sharding import PartitionSpec as P

HEADS = 16
TILE = 256
LANES = 128
AXES = ("img", "tile")
BF = jnp.bfloat16
F32 = jnp.float32


def nt(a, b):
    return lax.dot_general(a, b, (((1,), (1,)), ((), ())), preferred_element_type=F32)


def tn(a, b):
    return lax.dot_general(a, b, (((0,), (0,)), ((), ())), preferred_element_type=F32)


def nn(a, b):
    return jnp.dot(a, b, preferred_element_type=F32)


def attention_kernel(q_ref, d_ref, k_ref, v_ref, o_ref, dq_ref, dk_ref, dv_ref):
    width = q_ref.shape[1]
    size = width // HEADS
    scale = size ** (-0.5)

    def put(ref, first, cols, inside, value):
        value = value.astype(ref.dtype)
        if first:
            value = jnp.where(inside, value, ref[:, cols])
        ref[:, cols] = value

    for head in range(HEADS):
        low = head * size // LANES * LANES
        high = -(-(head + 1) * size // LANES) * LANES
        first = head * size - low
        cols = slice(low, high)
        lane = lax.broadcasted_iota(jnp.int32, (1, high - low), 1)
        inside = lane >= first
        mine = inside & (lane < first + size)
        q = jnp.where(mine, q_ref[:, cols], jnp.zeros((), BF))
        d = jnp.where(mine, d_ref[:, cols], jnp.zeros((), BF))
        k = k_ref[:, cols]
        v = v_ref[:, cols]
        scores = nt(q, k) * scale
        top = jnp.max(scores, axis=-1, keepdims=True)
        expo = jnp.exp(scores - top)
        probs = expo * (1.0 / jnp.sum(expo, axis=-1, keepdims=True))
        pb = probs.astype(BF)
        put(o_ref, first, cols, inside, nn(pb, v))
        dprob = nt(d, v)
        delta = jnp.sum(probs * dprob, axis=-1, keepdims=True)
        ds = (probs * (dprob - delta) * scale).astype(BF)
        put(dq_ref, first, cols, inside, nn(ds, k))
        put(dk_ref, first, cols, inside, tn(ds, q))
        put(dv_ref, first, cols, inside, tn(pb, d))


def attention(q, d, k, v):
    rows, width = q.shape
    keyrows = k.shape[0]
    vmem = pl.BlockSpec(memory_space=pltpu.VMEM)
    flops = 12 * rows * keyrows * width
    return pl.pallas_call(
        attention_kernel,
        out_shape=(
            jax.ShapeDtypeStruct((rows, width), BF),
            jax.ShapeDtypeStruct((rows, width), BF),
            jax.ShapeDtypeStruct((keyrows, width), BF),
            jax.ShapeDtypeStruct((keyrows, width), BF),
        ),
        in_specs=[vmem] * 4,
        out_specs=(vmem,) * 4,
        compiler_params=pltpu.CompilerParams(vmem_limit_bytes=40 * 2**20),
        cost_estimate=pl.CostEstimate(
            flops=4 * flops,
            bytes_accessed=2 * (4 * rows + 4 * keyrows) * width,
            transcendentals=HEADS * rows * keyrows,
        ),
        name="attention",
    )(q, d, k, v)


def on_device(n_img, n_tile, tiles, tile_image, guide, gain, w_query, w_key, w_value, w_out, grad_out):
    width = tiles.shape[1]
    images, part = guide.shape[0], guide.shape[1]
    i = lax.axis_index("img")
    t = lax.axis_index("tile")
    image = tile_image[0]
    tile_bits = [1 << b for b in range(n_tile.bit_length() - 1)]
    img_bits = [1 << b for b in range(n_img.bit_length() - 1)]

    def swap_tile(x, bit):
        return lax.ppermute(x, "tile", [(s, s ^ bit) for s in range(n_tile)])

    def swap_img(x, bit):
        return lax.ppermute(x, "img", [(s, s ^ bit) for s in range(n_img)])

    def pick(arr, which):
        chosen = arr[0]
        for c in range(1, images):
            chosen = jnp.where(which == c, arr[c], chosen)
        return chosen

    exchange = tile_bits[1:] + tile_bits[:1]
    codes = [0]
    for bit in reversed(exchange):
        codes = codes + [c | bit for c in codes]
    theirs = swap_tile(tile_image, 1)[0]
    first_image = swap_tile(tile_image, exchange[0])[0]
    pieces = {}
    for code in sorted((c for c in range(0, n_tile, 2)), key=lambda c: (c != 0, -c)):
        block = swap_tile(guide, code) if code else guide
        pieces[code] = pick(block, image)
        pieces[code | 1] = swap_tile(pick(block, theirs), 1)
    used = jnp.concatenate([pieces[c] for c in codes], axis=0)

    xf = tiles.astype(F32)
    rstd = lax.rsqrt(jnp.mean(xf * xf, axis=-1, keepdims=True) + 1e-06)
    normed = xf * rstd
    hidden = (normed * gain).astype(BF)
    r = width // (n_img * n_tile)
    order = np.arange(width).reshape(n_img // 2, 2, n_tile // 2, 2, r).transpose(1, 3, 0, 2, 4)
    order = jnp.asarray(order.reshape(2, -1), jnp.int32)
    core = i & 1

    def ordered(x, which):
        rows = lax.dynamic_index_in_dim(order, which, 0, keepdims=True)
        places = lax.broadcasted_iota(jnp.int32, (width, width // 2), 0)
        return nn(x, (places == rows).astype(BF)).astype(BF)

    query = nn(hidden, w_query).astype(BF)
    dout = nt(grad_out, w_out).astype(BF)
    hidden_send, hidden_keep = ordered(hidden, 1 - core), ordered(hidden, core)
    query, dout, hidden_send, hidden_keep, first_image = lax.optimization_barrier(
        (query, dout, hidden_send, hidden_keep, first_image)
    )
    keys = nn(used, w_key).astype(BF)
    values = nn(used, w_value).astype(BF)
    outv, dq, dk, dv = attention(query, dout, keys, values)

    def halve(x, axis, bit, swap):
        keep = lax.dynamic_index_in_dim(x, bit, axis, keepdims=False)
        send = lax.dynamic_index_in_dim(x, 1 - bit, axis, keepdims=False)
        return (keep.astype(F32) + swap(send).astype(F32)).astype(BF)

    def after(x, *done):
        return lax.optimization_barrier((x,) + done)[0]

    send_out = tn(ordered(outv, 1 - core), grad_out).astype(BF)
    send_query = tn(hidden_send, after(dq, send_out)).astype(BF)
    used_send = ordered(after(used, send_query), 1 - core)
    send_key = tn(used_send, dk).astype(BF)
    send_value = tn(used_send, after(dv, send_key)).astype(BF)

    def kept(left, right, sent):
        total = tn(left, right) + swap_img(sent, 1).astype(F32)
        return total.astype(BF).reshape(2, n_img // 2, width // (2 * n_img), width)

    out_keep = ordered(after(outv, send_value), core)
    used_keep = ordered(after(used, send_value), core)
    half_out = kept(out_keep, grad_out, send_out)
    half_key = kept(used_keep, dk, send_key)
    half_query = kept(hidden_keep, after(dq, send_value), send_query)
    half_value = kept(used_keep, dv, send_value)

    def over_tile(x):
        return halve(x, 1, t & 1, lambda s: swap_tile(s, 1))

    def over_img(x):
        for bit in img_bits[1:]:
            shape = x.shape
            x = x.reshape(shape[:-3] + (shape[-3] // 2, 2) + shape[-2:])
            x = halve(x, x.ndim - 3, (i // bit) & 1, lambda s, bit=bit: swap_img(s, bit))
        return x.reshape(x.shape[:-3] + x.shape[-2:])

    pair_a = jnp.stack([half_out, half_key])
    pair_b = jnp.stack([half_query, half_value])
    dq, dk, dv = (after(x, pair_a, pair_b) for x in (dq, dk, dv))
    pair_a, pair_b = over_img(pair_a), over_tile(pair_b)
    pair_a, pair_b = over_tile(pair_a), over_img(pair_b)

    four = jnp.stack([pair_b[0], pair_a[1], pair_b[1], pair_a[0]])
    four = four.reshape(4, n_tile // 2, r, width)
    grad_weights = lax.dynamic_index_in_dim(four, t // 2, 1, keepdims=False).astype(F32)
    for code in range(n_tile - 2, 0, -2):
        send = lax.dynamic_index_in_dim(four, (t ^ code) // 2, 1, keepdims=False)
        grad_weights = grad_weights + swap_tile(send, code).astype(F32)

    term = (nt(dk, w_key) + nt(dv, w_value)).astype(BF).reshape(n_tile, part, width)
    half = n_tile // 2
    received = swap_tile(term[half:], exchange[0]).astype(F32)
    own = term[:half].astype(F32)
    x = jnp.stack(
        [
            jnp.where(image == c, own, 0.0) + jnp.where(first_image == c, received, 0.0)
            for c in range(images)
        ],
        axis=1,
    ).astype(BF)
    for bit in exchange[1:]:
        half = x.shape[0] // 2
        x = (x[:half].astype(F32) + swap_tile(x[half:], bit).astype(F32)).astype(BF)
    grad_guide = x.reshape(guide.shape)

    dh = nt(dq, w_query)
    grad_gain = jnp.sum(dh * normed, axis=0)
    grad_gain = grad_gain + swap_img(grad_gain, 1)
    for bit in tile_bits[1:]:
        grad_gain = grad_gain + swap_tile(grad_gain, bit)
    grad_gain = after(grad_gain, four)
    grad_gain = grad_gain + swap_tile(grad_gain, 1)
    for bit in img_bits[1:]:
        grad_gain = grad_gain + swap_img(grad_gain, bit)
    dn = dh * gain
    grad_tiles = (rstd * (dn - normed * jnp.mean(dn * normed, axis=-1, keepdims=True))).astype(BF)
    return (grad_tiles, grad_guide, grad_weights, grad_gain)


def solution(mesh):
    return jax.shard_map(
        functools.partial(on_device, mesh.shape["img"], mesh.shape["tile"]),
        mesh=mesh,
        in_specs=(
            P(("img", "tile"), None),
            P(("img", "tile")),
            P("img", "tile", None),
            P(),
            P(),
            P(),
            P(),
            P(),
            P(("img", "tile"), None),
        ),
        out_specs=(
            P(("img", "tile"), None),
            P("img", "tile", None),
            P(None, ("img", "tile"), None),
            P(),
        ),
        check_vma=False,
    )
```
